256 devices in a mesh: fsdp: 256 (over x, y, z, core).
Axes of the slice: x: 4, y: 4, z: 8, core: 2. Of those that a mesh axis runs over, the one named last changes fastest.
Arguments:
- grads: bfloat16 [256, 20736, 128], P('fsdp'), may hold values from -15000 to 15000
- params: float32 [20736, 128], P('fsdp'), may hold values from -0.1875 to 0.1875
- moment: float32 [20736, 128], P('fsdp'), may hold values from -6 to 6
- second: float32 [20736, 128], P('fsdp'), may hold values from 0.1 to 4
- teacher: float32 [20736, 128], P('fsdp'), may hold values from -0.1875 to 0.1875
Outputs:
- params_out: float32 [20736, 128], P('fsdp')
- moment_out: float32 [20736, 128], P('fsdp')
- second_out: float32 [20736, 128], P('fsdp')
- teacher_out: float32 [20736, 128], P('fsdp')
- weights_out: bfloat16 [20736, 128], replicated
The draws below stay inside these ranges and needn't reach their ends.
All inputs are finite; a program needn't handle non-finite values.
Results may differ from the reference program's by a relative error of at most 0.001.
Values may be sent and summed in bfloat16 or wider, within the bound.
No kernel may reach another device: no remote copies, remote signals or barrier semaphores. Data moves between devices by JAX's collectives and lax.ppermute only.
A program may use at most 128 MiB of HBM per device.

```python
import math
import jax
import jax.numpy as jnp
from jax import lax

D = 1152
ROWS = 20736
N_FSDP = 256


def draw_grads(key, part):
    keys = jax.random.split(jax.random.fold_in(key, 17), 6)
    positions = jnp.arange(ROWS, dtype=jnp.float32)
    rising = jnp.exp(jnp.log(3.0) * positions / ROWS)[:, None]
    row_spread = jnp.exp(jax.random.uniform(keys[0], (ROWS, 1), jnp.float32) * jnp.log(10.0))
    col_spread = jnp.exp(jax.random.uniform(keys[1], (1, 128), jnp.float32) * jnp.log(10.0))
    pairing = jax.random.permutation(keys[5], N_FSDP).astype(jnp.int32)
    block_of_row = (jnp.arange(ROWS, dtype=jnp.int32) // (ROWS // N_FSDP)).astype(jnp.int32)
    boost = jnp.where(block_of_row[None, :] == pairing[:, None], 8.0, 1.0).astype(jnp.float32)[:, :, None]
    noise = jnp.clip(jax.random.normal(keys[4], (N_FSDP, ROWS, 128), jnp.float32), -5.0, 5.0)
    return (noise * boost * rising * row_spread * col_spread).astype(jnp.bfloat16)


def level_of(stream_key, shape, cuts, low, top_value):
    level, own = 1.0, jax.random.fold_in(stream_key, 6)
    for dim, parts in cuts:
        steps = jnp.exp(jax.random.uniform(jax.random.fold_in(own, dim), (parts,), jnp.float32, low / len(cuts), top_value / len(cuts)))
        level = level * jnp.repeat(steps, shape[dim] // parts).reshape([-1 if axis == dim else 1 for axis in range(len(shape))])
    return level


def scatter_about(key, dims, scale, reach, pieces=(), held_as=jnp.bfloat16):
    loudness = level_of(key, dims, pieces, -0.22, 0.18) if pieces else 1.0
    values = jax.random.normal(key, dims, jnp.float32) * scale * loudness
    return jnp.minimum(jnp.maximum(values, -reach), reach).astype(held_as)


def setup_inputs(seed: int = 0) -> dict:
    key_of = jax.random.split(jax.random.key(seed), 6)
    return {
        "grads": draw_grads(jax.random.fold_in(key_of[5], 71), 0),
        "params": scatter_about(key_of[1], (ROWS, 128), D ** -0.5, 0.1875, ((0, 256),), jnp.float32),
        "moment": scatter_about(key_of[2], (ROWS, 128), 1.0, 6.0, ((0, 256),), jnp.float32),
        "second": jnp.clip(jnp.exp(math.log(4.0) - 3.6888794 * jax.random.uniform(key_of[3], (ROWS, 128), jnp.float32) ** level_of(key_of[3], (ROWS, 128), ((0, 256),), -0.2, 0.2)), 0.1, 4.0),
        "teacher": scatter_about(key_of[4], (ROWS, 128), D ** -0.5, 0.1875, ((0, 256),), jnp.float32),
    }


def reference(grads, params, moment, second, teacher):

    def accumulate(total, piece):
        return (total + piece.astype(jnp.float32), None)
    summed, _ = lax.scan(accumulate, jnp.zeros(grads.shape[1:], jnp.float32), grads)
    squares = jnp.sum(summed * summed)
    entries = grads.shape[1] * grads.shape[2]
    factor = 1.0 / jnp.sqrt(squares / jnp.float32(entries) + 1e-06)
    clipped = factor * summed
    moment_out = 0.9 * moment + 0.1 * clipped
    second_out = 0.95 * second + 0.05 * clipped * clipped
    first_fix = 1.0 - 0.9 ** 10
    second_fix = 1.0 - 0.95 ** 10
    update = moment_out / first_fix / (jnp.sqrt(second_out / second_fix) + 1e-08) + 0.1 * params
    params_out = params - 0.001 * update
    teacher_out = 0.9999 * teacher + 0.0001 * params_out
    weights_out = params_out.astype(jnp.bfloat16)
    return (params_out, moment_out, second_out, teacher_out, weights_out)
```

```python
import jax
import jax.numpy as jnp
from jax import lax
from jax.experimental import pallas as pl
from jax.experimental.pallas import tpu as pltpu
from jax.sharding import Mesh
from jax.sharding import PartitionSpec as P

AXES = ("x", "y", "z", "c")
NX, NZ = 4, 8
OWN = 81
HALF = 8 * OWN
VMEM = 48 * 2**20
F32, BF16 = jnp.float32, jnp.bfloat16


def flat(x, y, z, c):
    return ((x * NX + y) * NZ + z) * 2 + c


def perm_of(step):
    everyone = [(x, y, z, c) for x in range(NX) for y in range(NX) for z in range(NZ) for c in range(2)]
    return [(flat(*d), flat(*step(*d))) for d in everyone]


def ring(level, r):
    def step(x, y, z, c):
        if c == level:
            return (x + r) % NX, y, z, c
        return x, (y + r) % NX, z, c

    return perm_of(step)


def to_owner(r):
    def step(x, y, z, c):
        j = (z + r) % 8
        return x, y, 4 * c + j // 2, j % 2

    return perm_of(step)


COLUMN = [perm_of(lambda x, y, z, c, k=k: (x, y, (z + k // 2) % NZ, (c + k) % 2)) for k in range(1, 2 * NZ)]
PLANE = [perm_of(lambda x, y, z, c, k=k: ((x + k // NX) % NX, (y + k) % NX, z, c)) for k in range(1, NX * NX)]
SWAP = perm_of(lambda x, y, z, c: (x, y, z, 1 - c))
RINGS = [[ring(level, r) for r in range(NX)] for level in range(2)]
OWNERS = [to_owner(r) for r in range(8)]
HOLDERS = [[(b, a) for a, b in pairs] for pairs in OWNERS]


def send(x, perm):
    return lax.ppermute(x, AXES, perm)


def over_column(v):
    return sum([send(v, pairs) for pairs in COLUMN], v)


def over_plane(v):
    return sum([send(v, pairs) for pairs in PLANE], v)


def call(kernel, grid, ins, outs, ids, arrays, cost, scratch=()):
    return pl.pallas_call(
        kernel,
        grid_spec=pltpu.PrefetchScalarGridSpec(
            num_scalar_prefetch=1, grid=grid, in_specs=ins, out_specs=outs[0], scratch_shapes=list(scratch)
        ),
        out_shape=outs[1],
        compiler_params=pltpu.CompilerParams(vmem_limit_bytes=VMEM),
        cost_estimate=pl.CostEstimate(flops=cost, bytes_accessed=cost, transcendentals=0),
    )(ids, *arrays)


def sum_pair(ids, mine, theirs, r):
    def kernel(ids_ref, a_ref, b_ref, o_ref):
        total = a_ref[0, 0, 0].astype(F32) + b_ref[0, 0].astype(F32)
        o_ref[0] = total.astype(BF16)

    def at(j, ids):
        first = lax.rem(ids[1] + r, NX)
        on_x = ids[0] == 0
        return jnp.where(on_x, first, j), jnp.where(on_x, j, first)

    ins = [
        pl.BlockSpec((1, 1, 1, HALF, 128), lambda j, ids: (*at(j, ids), ids[0], 0, 0)),
        pl.BlockSpec((1, 1, HALF, 128), lambda j, ids: (*at(j, ids), 0, 0)),
    ]
    out = pl.BlockSpec((1, HALF, 128), lambda j, ids: (j, 0, 0)), jax.ShapeDtypeStruct((NX, HALF, 128), BF16)
    return call(kernel, (NX,), ins, out, ids, (mine, theirs), 2_000_000)


def own_specs(q):
    def at(i, ids):
        second = lax.rem(ids[2] + q, NX)
        on_x = ids[0] == 0
        return jnp.where(on_x, ids[1], second), jnp.where(on_x, second, ids[1])

    return [
        pl.BlockSpec((1, 1, 1, HALF, 128), lambda i, ids: (*at(i, ids), ids[0], 0, 0)),
        pl.BlockSpec((1, 1, HALF, 128), lambda i, ids: (*at(i, ids), 0, 0)),
    ] + [pl.BlockSpec((1, HALF, 128), lambda i, ids: (lax.rem(ids[2] + q, NX), 0, 0))] * 3


def ring_total(a_ref, b_ref, c_ref, d_ref, e_ref):
    total = a_ref[0, 0, 0].astype(F32) + b_ref[0, 0].astype(F32)
    return total + c_ref[0].astype(F32) + d_ref[0].astype(F32) + e_ref[0].astype(F32)


def sum_ring(ids, terms, q):
    def kernel(ids_ref, *refs):
        refs[-1][...] = ring_total(*refs[:-1])

    out = pl.BlockSpec((HALF, 128), lambda i, ids: (0, 0)), jax.ShapeDtypeStruct((HALF, 128), F32)
    return call(kernel, (1,), own_specs(q), out, ids, terms, 1_000_000)


def sum_plane(ids, terms, got):
    def kernel(ids_ref, *refs):
        outs, total = refs[8:16], refs[16]
        total[...] = ring_total(*refs[:5]) + refs[5][...] + refs[6][...] + refs[7][...]
        for r in range(8):
            j = lax.rem(ids_ref[3] + r, 8)
            outs[r][...] = total[pl.ds(j * OWN, OWN), :]

    whole = pl.BlockSpec((HALF, 128), lambda i, ids: (0, 0))
    out = (
        [pl.BlockSpec((OWN, 128), lambda i, ids: (0, 0))] * 8,
        [jax.ShapeDtypeStruct((OWN, 128), F32)] * 8,
    )
    scratch = (pltpu.VMEM((HALF, 128), F32),)
    return call(kernel, (1,), own_specs(0) + [whole] * 3, out, ids, (*terms, *got), 2_000_000, scratch)


def join(ids, pieces):
    def kernel(ids_ref, *refs):
        out, total = refs[8], refs[9]
        for r in range(8):
            j = lax.rem(ids_ref[3] + r, 8)
            total[pl.ds(j * OWN, OWN), :] = refs[r][...].astype(F32)
        out[...] = total[...].astype(BF16)

    out = pl.BlockSpec((HALF, 128), lambda i, ids: (0, 0)), jax.ShapeDtypeStruct((HALF, 128), BF16)
    scratch = (pltpu.VMEM((HALF, 128), F32),)
    ins = [pl.BlockSpec((OWN, 128), lambda i, ids: (0, 0))] * 8
    return call(kernel, (1,), ins, out, ids, pieces, 300_000, scratch)


def stack(blocks):
    def kernel(ids_ref, *refs):
        for k in range(3):
            refs[3][k] = refs[k][...]

    whole = pl.BlockSpec((HALF, 128), lambda i, ids: (0, 0))
    out = pl.BlockSpec((3, HALF, 128), lambda i, ids: (0, 0, 0)), jax.ShapeDtypeStruct((3, HALF, 128), BF16)
    return call(kernel, (1,), [whole] * 3, out, jnp.zeros((1,), jnp.int32), blocks, 1_000_000)


def place(ids, kinds, arrays):
    jobs = [(k, n) for k, kind in enumerate(kinds) for n in range(len(kind[2]))]

    def kernel(ids_ref, *refs):
        out, sems = refs[-2], refs[-1]
        copies = []
        for s, (k, n) in enumerate(jobs):
            swapped, r, shifts = kinds[k]
            core = ids_ref[0] if swapped == 0 else 1 - ids_ref[0]
            x = lax.rem(ids_ref[4] + jnp.where(core == 0, r, shifts[n]), NX)
            y = lax.rem(ids_ref[5] + jnp.where(core == 0, shifts[n], r), NX)
            src = refs[k] if len(shifts) == 1 else refs[k].at[n]
            copies.append(pltpu.make_async_copy(src, out.at[x, y, core], sems.at[s]))
        for copy in copies:
            copy.start()
        for copy in copies:
            copy.wait()

    anywhere = pl.BlockSpec(memory_space=pl.ANY)
    out = anywhere, jax.ShapeDtypeStruct((NX, NX, 2, HALF, 128), BF16)
    sems = (pltpu.SemaphoreType.DMA((len(jobs),)),)
    return call(kernel, (1,), [anywhere] * len(arrays), out, ids, arrays, 10_000_000, sems)


def body(grads, params, moment, second, teacher):
    x, y, z, c = (lax.axis_index(a) for a in AXES)
    ids = jnp.stack([c, jnp.where(c == 0, x, y), jnp.where(c == 0, y, x), z, x, y]).astype(jnp.int32)

    mine = grads.reshape(NX, NX, 2, HALF, 128)
    theirs = send(lax.dynamic_index_in_dim(mine, 1 - c, 2, keepdims=False), SWAP)
    got = [send(sum_pair(ids, mine, theirs, r), RINGS[0][r]) for r in (2, 1, 3)]
    terms = (mine, theirs, *got)
    got = [send(sum_ring(ids, terms, q), RINGS[1][q]) for q in (2, 1, 3)]
    pieces = sum_plane(ids, terms, got)
    got = [send(pieces[r], OWNERS[r]) for r in range(8)]
    summed = sum(got[1:], got[0])

    squares = jnp.sum(over_plane(over_column(jnp.sum(summed * summed, axis=0, keepdims=True))))
    entries = grads.shape[1] * grads.shape[2]
    factor = 1.0 / jnp.sqrt(squares / jnp.float32(entries) + 1e-06)
    clipped = factor * summed
    moment_out = 0.9 * moment + 0.1 * clipped
    second_out = 0.95 * second + 0.05 * clipped * clipped
    first_fix = 1.0 - 0.9**10
    second_fix = 1.0 - 0.95**10
    update = moment_out / first_fix / (jnp.sqrt(second_out / second_fix) + 1e-08) + 0.1 * params
    params_out = params - 0.001 * update
    teacher_out = 0.9999 * teacher + 0.0001 * params_out

    weights = params_out.astype(BF16)
    block = join(ids, [send(weights, HOLDERS[r]) for r in range(8)])
    across = [send(block, RINGS[1][r]) for r in (2, 1, 3)]
    row = stack(across)
    near = [block] + [send(block, RINGS[0][r]) for r in (2, 1, 3)]
    far = [row] + [send(row, RINGS[0][r]) for r in (2, 1, 3)]
    arrays, kinds = [], []
    for r, a, b in zip((0, 2, 3, 1), near, far):
        for swapped in (0, 1):
            kinds += [(swapped, r, (0,)), (swapped, r, (2, 3, 1))]
            arrays += [a, b] if not swapped else [send(a, SWAP), send(b, SWAP)]
    weights_out = place(ids, kinds, arrays).reshape(grads.shape[1:])
    return (params_out, moment_out, second_out, teacher_out, weights_out)


def solution(mesh):
    split = Mesh(mesh.devices.reshape(NX, NX, NZ, 2), AXES)
    in_specs = (P(AXES, None, None), P(AXES, None), P(AXES, None), P(AXES, None), P(AXES, None))
    out_specs = (P(AXES, None), P(AXES, None), P(AXES, None), P(AXES, None), P())
    return jax.shard_map(body, mesh=split, in_specs=in_specs, out_specs=out_specs, check_vma=False)
```

```python
import jax
import jax.numpy as jnp
from jax import lax
from jax.experimental import pallas as pl
from jax.experimental.pallas import tpu as pltpu
from jax.sharding import Mesh
from jax.sharding import PartitionSpec as P

AXES = ("x", "y", "z", "c")
NX, NZ = 4, 8
OWN = 81
HALF = 8 * OWN
VMEM = 32 * 2**20
F32, BF16 = jnp.float32, jnp.bfloat16


def flat(x, y, z, c):
    return ((x * NX + y) * NZ + z) * 2 + c


def perm_of(step):
    everyone = [(x, y, z, c) for x in range(NX) for y in range(NX) for z in range(NZ) for c in range(2)]
    return [(flat(*d), flat(*step(*d))) for d in everyone]


def ring(level, r):
    def step(x, y, z, c):
        if c == level:
            return (x + r) % NX, y, z, c
        return x, (y + r) % NX, z, c

    return perm_of(step)


def owner(x, y, z, c):
    return x, y, 4 * c + z // 2, z % 2


SWAP = perm_of(lambda x, y, z, c: (x, y, z, 1 - c))
RINGS = [[ring(level, r) for r in range(NX)] for level in range(2)]
TO_OWNER = perm_of(owner)
TO_HOLDER = [(b, a) for a, b in TO_OWNER]
SHIFTS = (2, 1, 3)


def send(x, perm):
    return lax.ppermute(x, AXES, perm)


def exchange(x, axes):
    return lax.all_to_all(x, axes, split_axis=0, concat_axis=0, tiled=True)


def call(kernel, ins, outs, arrays, cost, scratch=(), aliases=None):
    spaces = {"s": pltpu.SMEM, "v": pltpu.VMEM, "a": pl.ANY}
    return pl.pallas_call(
        kernel,
        in_specs=[pl.BlockSpec(memory_space=spaces[k]) for k in ins],
        out_specs=[pl.BlockSpec(memory_space=spaces[k]) for k, _, _ in outs],
        out_shape=[jax.ShapeDtypeStruct(shape, dtype) for _, shape, dtype in outs],
        scratch_shapes=list(scratch),
        input_output_aliases=aliases or {},
        compiler_params=pltpu.CompilerParams(vmem_limit_bytes=VMEM),
        cost_estimate=pl.CostEstimate(flops=cost, bytes_accessed=cost, transcendentals=0),
    )(*arrays)


def pick(ids, mine, r):
    def kernel(ids_ref, mine_ref, give_ref, keep_ref, sems):
        copies = []
        for k, (core, out) in enumerate(((1 - ids_ref[0], give_ref), (ids_ref[0], keep_ref))):
            on_x = core == 0
            first = lax.rem(jnp.where(on_x, ids_ref[4], ids_ref[5]) + r, NX)
            for j in range(NX):
                at = jnp.where(on_x, first, j), jnp.where(on_x, j, first)
                copies.append(pltpu.make_async_copy(mine_ref.at[at[0], at[1], core], out.at[j], sems.at[4 * k + j]))
        for copy in copies:
            copy.start()
        for copy in copies:
            copy.wait()

    out = ("v", (NX, HALF, 128), BF16)
    return call(kernel, "sa", [out, out], (ids, mine), 2_000_000, (pltpu.SemaphoreType.DMA((8,)),))


def sum_pair(keep, theirs, dtype):
    def kernel(a_ref, b_ref, o_ref):
        @pl.loop(0, NX)
        def _(j):
            o_ref[j] = (a_ref[j].astype(F32) + b_ref[j].astype(F32)).astype(dtype)

    return call(kernel, "vv", [("v", (NX, HALF, 128), dtype)], (keep, theirs), 1_000_000)[0]


def ring_total(j, refs):
    total = refs[0][j]
    for ref in refs[1:]:
        total = total + ref[j].astype(F32)
    return total


def sum_ring(ids, terms, q):
    def kernel(ids_ref, *refs):
        refs[-1][...] = ring_total(lax.rem(ids_ref[2] + q, NX), refs[:-1])

    return call(kernel, "s" + "v" * 4, [("v", (HALF, 128), F32)], (ids, *terms), 500_000)[0]


def sum_plane(ids, terms, got):
    def kernel(ids_ref, *refs):
        out, total = refs[-2:]
        total[...] = ring_total(ids_ref[2], refs[:4]) + refs[4][...] + refs[5][...] + refs[6][...]
        for j in range(8):
            out[j] = total[j * OWN : (j + 1) * OWN, :]

    out = [("v", (8, OWN, 128), F32)]
    scratch = (pltpu.VMEM((HALF, 128), F32),)
    return call(kernel, "s" + "v" * 7, out, (ids, *terms, *got), 1_000_000, scratch)[0]


def join(pieces):
    def kernel(in_ref, out, total):
        for j in range(8):
            total[j * OWN : (j + 1) * OWN, :] = in_ref[j].astype(F32)
        out[...] = total[...].astype(BF16)

    return call(kernel, "v", [("v", (HALF, 128), BF16)], (pieces,), 300_000, (pltpu.VMEM((HALF, 128), F32),))[0]


def stack(blocks):
    def kernel(*refs):
        for k in range(3):
            refs[3][k] = refs[k][...]

    return call(kernel, "vvv", [("v", (3, HALF, 128), BF16)], blocks, 500_000)[0]


def place(ids, kinds, arrays, out=None):
    jobs = [(k, n) for k, kind in enumerate(kinds) for n in range(len(kind[2]))]

    def kernel(ids_ref, *refs):
        out_ref, sems = refs[-2], refs[-1]
        copies = []
        for s, (k, n) in enumerate(jobs):
            swapped, r, shifts = kinds[k]
            core = ids_ref[0] if swapped == 0 else 1 - ids_ref[0]
            x = lax.rem(ids_ref[4] + jnp.where(core == 0, r, shifts[n]), NX)
            y = lax.rem(ids_ref[5] + jnp.where(core == 0, shifts[n], r), NX)
            src = refs[k] if len(shifts) == 1 else refs[k].at[n]
            copies.append(pltpu.make_async_copy(src, out_ref.at[x, y, core], sems.at[s]))
        for copy in copies:
            copy.start()
        for copy in copies:
            copy.wait()

    more = () if out is None else (out,)
    aliases = {} if out is None else {1 + len(arrays): 0}
    sems = (pltpu.SemaphoreType.DMA((len(jobs),)),)
    outs = [("a", (NX, NX, 2, HALF, 128), BF16)]
    return call(kernel, "s" + "a" * (len(arrays) + len(more)), outs, (ids, *arrays, *more), 5_000_000, sems, aliases)[0]


def adamw(factor, summed, params, moment, second):
    clipped = factor * summed
    moment_out = 0.9 * moment + 0.1 * clipped
    second_out = 0.95 * second + 0.05 * clipped * clipped
    first_fix = 1.0 - 0.9**10
    second_fix = 1.0 - 0.95**10
    update = moment_out / first_fix / (jnp.sqrt(second_out / second_fix) + 1e-08) + 0.1 * params
    return params - 0.001 * update, moment_out, second_out


def body(grads, params, moment, second, teacher):
    x, y, z, c = (lax.axis_index(a) for a in AXES)
    ids = jnp.stack([c, jnp.where(c == 0, x, y), jnp.where(c == 0, y, x), z, x, y]).astype(jnp.int32)

    mine = grads.reshape(NX, NX, 2, HALF, 128)
    picked = [pick(ids, mine, r) for r in (*SHIFTS, 0)]
    theirs = [send(give, SWAP) for give, _ in picked]
    got = [send(sum_pair(picked[k][1], theirs[k], BF16), RINGS[0][r]) for k, r in enumerate(SHIFTS)]
    terms = (sum_pair(picked[3][1], theirs[3], F32), *got)
    got = [send(sum_ring(ids, terms, q), RINGS[1][q]) for q in SHIFTS]
    held = jnp.sum(exchange(sum_plane(ids, terms, got), "z"), axis=0)
    summed = send(held, TO_OWNER)
    state = send(jnp.stack([params, moment, second]), TO_HOLDER)

    partial = jnp.sum(held * held, axis=0, keepdims=True)
    everyone = NX * NX * NZ * 2
    squares = jnp.sum(exchange(jnp.broadcast_to(partial, (everyone, 128)), AXES))
    entries = grads.shape[1] * grads.shape[2]
    factor = 1.0 / jnp.sqrt(squares / jnp.float32(entries) + 1e-06)

    weights = adamw(factor, held, *state)[0].astype(BF16)
    block = join(exchange(jnp.broadcast_to(weights, (8, OWN, 128)), "z"))
    across = [send(block, RINGS[1][r]) for r in SHIFTS]
    near = [send(block, RINGS[0][r]) for r in SHIFTS]
    row = stack(across)
    far = [send(row, RINGS[0][r]) for r in SHIFTS]
    back = tuple((NX - r) % NX for r in SHIFTS)
    kinds = [(0, (0,)), (0, back)] + [(r, (0,)) for r in back]
    first = [block, row, *near]
    out = place(
        ids,
        [(0, *kind) for kind in kinds] + [(1, *kind) for kind in kinds],
        first + [send(a, SWAP) for a in first],
    )
    kinds = [(r, back) for r in back]
    out = place(
        ids,
        [(0, *kind) for kind in kinds] + [(1, *kind) for kind in kinds],
        far + [send(a, SWAP) for a in far],
        out,
    )
    weights_out = out.reshape(grads.shape[1:])

    params_out, moment_out, second_out = adamw(factor, summed, params, moment, second)
    teacher_out = 0.9999 * teacher + 0.0001 * params_out
    return (params_out, moment_out, second_out, teacher_out, weights_out)


def solution(mesh):
    split = Mesh(mesh.devices.reshape(NX, NX, NZ, 2), AXES)
    in_specs = (P(AXES, None, None), P(AXES, None), P(AXES, None), P(AXES, None), P(AXES, None))
    out_specs = (P(AXES, None), P(AXES, None), P(AXES, None), P(AXES, None), P())
    return jax.shard_map(body, mesh=split, in_specs=in_specs, out_specs=out_specs, check_vma=False)
```

```python
import jax
import jax.numpy as jnp
from jax import lax
from jax.experimental import pallas as pl
from jax.experimental.pallas import tpu as pltpu
from jax.sharding import Mesh
from jax.sharding import PartitionSpec as P

AXES = ("x", "y", "z", "c")
NX, NZ = 4, 8
OWN = 81
HALF = 8 * OWN
MIB = 2**20
F32, BF16 = jnp.float32, jnp.bfloat16


def flat(x, y, z, c):
    return ((x * NX + y) * NZ + z) * 2 + c


def perm_of(step):
    everyone = [(x, y, z, c) for x in range(NX) for y in range(NX) for z in range(NZ) for c in range(2)]
    return [(flat(*d), flat(*step(*d))) for d in everyone]


def ring(level, r):
    def step(x, y, z, c):
        if c == level:
            return (x + r) % NX, y, z, c
        return x, (y + r) % NX, z, c

    return perm_of(step)


def owner(x, y, z, c):
    return x, y, 4 * c + z // 2, z % 2


SWAP = perm_of(lambda x, y, z, c: (x, y, z, 1 - c))
RINGS = [[ring(level, r) for r in range(NX)] for level in range(2)]
TO_OWNER = perm_of(owner)
TO_HOLDER = [(b, a) for a, b in TO_OWNER]
SHIFTS = (2, 1, 3)


def send(x, perm):
    return lax.ppermute(x, AXES, perm)


def exchange(x, axes):
    return lax.all_to_all(x, axes, split_axis=0, concat_axis=0, tiled=True)


def call(kernel, ins, outs, arrays, cost, scratch=(), aliases=None, vmem=24):
    spaces = {"s": pltpu.SMEM, "v": pltpu.VMEM, "a": pl.ANY, "h": pltpu.HBM}
    return pl.pallas_call(
        kernel,
        in_specs=[pl.BlockSpec(memory_space=spaces[k]) for k in ins],
        out_specs=[pl.BlockSpec(memory_space=spaces[k]) for k, _, _ in outs],
        out_shape=[jax.ShapeDtypeStruct(shape, dtype) for _, shape, dtype in outs],
        scratch_shapes=list(scratch),
        input_output_aliases=aliases or {},
        compiler_params=pltpu.CompilerParams(vmem_limit_bytes=vmem * MIB),
        cost_estimate=pl.CostEstimate(flops=cost, bytes_accessed=cost, transcendentals=0),
    )(*arrays)


def pick(ids, mine, shifts, give):
    def kernel(ids_ref, mine_ref, *refs):
        outs, sems = refs[:-1], refs[-1]
        core = 1 - ids_ref[0] if give else ids_ref[0]
        on_x = core == 0
        copies = []
        for k, r in enumerate(shifts):
            first = lax.rem(jnp.where(on_x, ids_ref[4], ids_ref[5]) + r, NX)
            for j in range(NX):
                at = jnp.where(on_x, first, j), jnp.where(on_x, j, first)
                copies.append(pltpu.make_async_copy(mine_ref.at[at[0], at[1], core], outs[k].at[j], sems.at[4 * k + j]))
        for copy in copies:
            copy.start()
        for copy in copies:
            copy.wait()

    outs = [("v", (NX, HALF, 128), BF16)] * len(shifts)
    sems = (pltpu.SemaphoreType.DMA((4 * len(shifts),)),)
    return call(kernel, "sh", outs, (ids, mine), 1_000_000 * len(shifts), sems, vmem=50 if give else 48)


def sum_pair(keep, theirs, dtype):
    def kernel(a_ref, b_ref, o_ref):
        @pl.loop(0, NX)
        def _(j):
            o_ref[j] = (a_ref[j].astype(F32) + b_ref[j].astype(F32)).astype(dtype)

    return call(kernel, "vv", [("v", (NX, HALF, 128), dtype)], (keep, theirs), 1_000_000)[0]


def ring_total(j, refs):
    total = refs[0][j]
    for ref in refs[1:]:
        total = total + ref[j].astype(F32)
    return total


def sum_ring(ids, terms, q):
    def kernel(ids_ref, *refs):
        refs[-1][...] = ring_total(lax.rem(ids_ref[2] + q, NX), refs[:-1])

    return call(kernel, "s" + "v" * 4, [("v", (HALF, 128), F32)], (ids, *terms), 500_000)[0]


def sum_plane(ids, terms, got):
    def kernel(ids_ref, *refs):
        out, total = refs[-2:]
        total[...] = ring_total(ids_ref[2], refs[:4]) + refs[4][...] + refs[5][...] + refs[6][...]
        for j in range(8):
            out[j] = total[j * OWN : (j + 1) * OWN, :]

    out = [("v", (8, OWN, 128), F32)]
    scratch = (pltpu.VMEM((HALF, 128), F32),)
    return call(kernel, "s" + "v" * 7, out, (ids, *terms, *got), 1_000_000, scratch)[0]


def join(pieces):
    def kernel(in_ref, out, total):
        for j in range(8):
            total[j * OWN : (j + 1) * OWN, :] = in_ref[j].astype(F32)
        out[...] = total[...].astype(BF16)

    return call(kernel, "v", [("v", (HALF, 128), BF16)], (pieces,), 300_000, (pltpu.VMEM((HALF, 128), F32),))[0]


def stack(*blocks):
    def kernel(*refs):
        for k in range(2):
            refs[2][k] = refs[k][...]

    return call(kernel, "vv", [("v", (2, HALF, 128), BF16)], blocks, 300_000)[0]


def place(ids, kinds, arrays, out=None):
    jobs = [(k, n) for k, kind in enumerate(kinds) for n in range(len(kind[2]))]

    def kernel(ids_ref, *refs):
        out_ref, sems = refs[-2], refs[-1]
        copies = []
        for s, (k, n) in enumerate(jobs):
            swapped, r, shifts = kinds[k]
            core = ids_ref[0] if swapped == 0 else 1 - ids_ref[0]
            x = lax.rem(ids_ref[4] + jnp.where(core == 0, r, shifts[n]), NX)
            y = lax.rem(ids_ref[5] + jnp.where(core == 0, shifts[n], r), NX)
            src = refs[k] if len(shifts) == 1 else refs[k].at[n]
            copies.append(pltpu.make_async_copy(src, out_ref.at[x, y, core], sems.at[s]))
        for copy in copies:
            copy.start()
        for copy in copies:
            copy.wait()

    more = () if out is None else (out,)
    aliases = {} if out is None else {1 + len(arrays): 0}
    sems = (pltpu.SemaphoreType.DMA((len(jobs),)),)
    outs = [("a", (NX, NX, 2, HALF, 128), BF16)]
    return call(kernel, "s" + "a" * (len(arrays) + len(more)), outs, (ids, *arrays, *more), 5_000_000, sems, aliases)[0]


def adamw(factor, summed, params, moment, second):
    clipped = factor * summed
    moment_out = 0.9 * moment + 0.1 * clipped
    second_out = 0.95 * second + 0.05 * clipped * clipped
    first_fix = 1.0 - 0.9**10
    second_fix = 1.0 - 0.95**10
    update = moment_out / first_fix / (jnp.sqrt(second_out / second_fix) + 1e-08) + 0.1 * params
    return params - 0.001 * update, moment_out, second_out


def body(grads, params, moment, second, teacher):
    x, y, z, c = (lax.axis_index(a) for a in AXES)
    ids = jnp.stack([c, jnp.where(c == 0, x, y), jnp.where(c == 0, y, x), z, x, y]).astype(jnp.int32)

    mine = grads.reshape(NX, NX, 2, HALF, 128)
    order = (*SHIFTS, 0)
    give = pick(ids, mine, order, True)
    theirs = [send(g, SWAP) for g in give]
    keep = pick(ids, mine, order, False)
    got = [send(sum_pair(keep[k], theirs[k], BF16), RINGS[0][r]) for k, r in enumerate(SHIFTS)]
    state = send(jnp.stack([params, moment, second]), TO_HOLDER)
    got[2], state = lax.optimization_barrier((got[2], state))
    terms = (sum_pair(keep[3], theirs[3], F32), *got)
    got = [send(sum_ring(ids, terms, q), RINGS[1][q]) for q in SHIFTS]
    held = jnp.sum(exchange(sum_plane(ids, terms, got), "z"), axis=0)
    summed = send(held, TO_OWNER)

    partial = jnp.sum(held * held, axis=0, keepdims=True)
    everyone = NX * NX * NZ * 2
    squares = jnp.sum(exchange(jnp.broadcast_to(partial, (everyone, 128)), AXES))
    squares, summed = lax.optimization_barrier((squares, summed))
    entries = grads.shape[1] * grads.shape[2]
    factor = 1.0 / jnp.sqrt(squares / jnp.float32(entries) + 1e-06)

    weights = adamw(factor, held, *state)[0].astype(BF16)
    block = join(exchange(jnp.broadcast_to(weights, (8, OWN, 128)), "z"))
    across = [send(block, RINGS[1][r]) for r in (1, 3, 2)]
    left, left_at = stack(block, across[0]), (0, 3)
    right, right_at = stack(across[1], across[2]), (1, 2)
    up, down = RINGS[0][3], RINGS[0][1]
    near = [send(left, up), send(right, down), send(right, up), send(left, down)]
    far = [send(near[0], up), send(near[1], down)]

    def both(r, at):
        return [(0, r, at), (1, r, at)]

    def pair(v):
        return [v, send(v, SWAP)]

    out = place(ids, both(0, left_at) + both(0, right_at), pair(left) + pair(right))
    near[2], near[3], out = lax.optimization_barrier((near[2], near[3], out))
    out = place(ids, both(1, left_at) + both(3, right_at), pair(near[0]) + pair(near[1]), out)
    far[0], far[1], out = lax.optimization_barrier((far[0], far[1], out))
    kinds = both(1, right_at) + both(3, left_at) + [(0, 2, left_at), (0, 2, right_at)]
    out = place(ids, kinds, pair(near[2]) + pair(near[3]) + far, out)
    out = place(ids, [(1, 2, left_at), (1, 2, right_at)], [send(v, SWAP) for v in far], out)
    weights_out = out.reshape(grads.shape[1:])

    params_out, moment_out, second_out = adamw(factor, summed, params, moment, second)
    teacher_out = 0.9999 * teacher + 0.0001 * params_out
    return (params_out, moment_out, second_out, teacher_out, weights_out)


def solution(mesh):
    split = Mesh(mesh.devices.reshape(NX, NX, NZ, 2), AXES)
    in_specs = (P(AXES, None, None), P(AXES, None), P(AXES, None), P(AXES, None), P(AXES, None))
    out_specs = (P(AXES, None), P(AXES, None), P(AXES, None), P(AXES, None), P())
    return jax.shard_map(body, mesh=split, in_specs=in_specs, out_specs=out_specs, check_vma=False)
```

```python
import jax
import jax.numpy as jnp
from jax import lax
from jax.experimental import pallas as pl
from jax.experimental.pallas import tpu as pltpu
from jax.sharding import Mesh
from jax.sharding import PartitionSpec as P

AXES = ("x", "y", "z", "c")
NX, NZ = 4, 8
OWN = 81
HALF = 8 * OWN
MIB = 2**20
F32, BF16 = jnp.float32, jnp.bfloat16


def flat(x, y, z, c):
    return ((x * NX + y) * NZ + z) * 2 + c


def perm_of(step):
    everyone = [(x, y, z, c) for x in range(NX) for y in range(NX) for z in range(NZ) for c in range(2)]
    return [(flat(*d), flat(*step(*d))) for d in everyone]


def ring(level, r):
    def step(x, y, z, c):
        if c == level:
            return (x + r) % NX, y, z, c
        return x, (y + r) % NX, z, c

    return perm_of(step)


def owner(x, y, z, c):
    return x, y, 4 * c + z // 2, z % 2


SWAP = perm_of(lambda x, y, z, c: (x, y, z, 1 - c))
RINGS = [[ring(level, r) for r in range(NX)] for level in range(2)]
TO_OWNER = perm_of(owner)
TO_HOLDER = [(b, a) for a, b in TO_OWNER]
SHIFTS = (2, 1, 3)


def send(x, perm):
    return lax.ppermute(x, AXES, perm)


def after(x, *others):
    return lax.optimization_barrier((x, *others))[0]


def exchange(x, axes):
    return lax.all_to_all(x, axes, split_axis=0, concat_axis=0, tiled=True)


def call(kernel, ins, outs, arrays, cost, scratch=(), aliases=None, vmem=24):
    spaces = {"s": pltpu.SMEM, "v": pltpu.VMEM, "a": pl.ANY, "h": pltpu.HBM}
    return pl.pallas_call(
        kernel,
        in_specs=[pl.BlockSpec(memory_space=spaces[k]) for k in ins],
        out_specs=[pl.BlockSpec(memory_space=spaces[k]) for k, _, _ in outs],
        out_shape=[jax.ShapeDtypeStruct(shape, dtype) for _, shape, dtype in outs],
        scratch_shapes=list(scratch),
        input_output_aliases=aliases or {},
        compiler_params=pltpu.CompilerParams(vmem_limit_bytes=vmem * MIB),
        cost_estimate=pl.CostEstimate(flops=cost, bytes_accessed=cost, transcendentals=0),
    )(*arrays)


def pick(ids, mine, shifts, give):
    def kernel(ids_ref, mine_ref, *refs):
        outs, sems = refs[:-1], refs[-1]
        core = 1 - ids_ref[0] if give else ids_ref[0]
        on_x = core == 0
        copies = []
        for k, r in enumerate(shifts):
            first = lax.rem(jnp.where(on_x, ids_ref[4], ids_ref[5]) + r, NX)
            for j in range(NX):
                at = jnp.where(on_x, first, j), jnp.where(on_x, j, first)
                copies.append(pltpu.make_async_copy(mine_ref.at[at[0], at[1], core], outs[k].at[j], sems.at[4 * k + j]))
        for copy in copies:
            copy.start()
        for copy in copies:
            copy.wait()

    outs = [("v", (NX, HALF, 128), BF16)] * len(shifts)
    sems = (pltpu.SemaphoreType.DMA((4 * len(shifts),)),)
    return call(kernel, "sh", outs, (ids, mine), 1_000_000 * len(shifts), sems, vmem=50 if give else 48)


def sum_pair(keep, theirs, dtype):
    def kernel(a_ref, b_ref, o_ref):
        @pl.loop(0, NX)
        def _(j):
            o_ref[j] = (a_ref[j].astype(F32) + b_ref[j].astype(F32)).astype(dtype)

    return call(kernel, "vv", [("v", (NX, HALF, 128), dtype)], (keep, theirs), 1_000_000)[0]


def ring_total(j, refs):
    total = refs[0][j]
    for ref in refs[1:]:
        total = total + ref[j].astype(F32)
    return total


def sum_ring(ids, terms):
    def kernel(ids_ref, *refs):
        for q, out in zip(SHIFTS, refs[4:]):
            out[...] = ring_total(lax.rem(ids_ref[2] + q, NX), refs[:4])

    return call(kernel, "s" + "v" * 4, [("v", (HALF, 128), F32)] * 3, (ids, *terms), 1_000_000)


def sum_plane(ids, terms, got):
    def kernel(ids_ref, *refs):
        out, total = refs[-2:]
        total[...] = ring_total(ids_ref[2], refs[:4]) + refs[4][...] + refs[5][...] + refs[6][...]
        for j in range(8):
            out[j] = total[j * OWN : (j + 1) * OWN, :]

    out = [("v", (8, OWN, 128), F32)]
    scratch = (pltpu.VMEM((HALF, 128), F32),)
    return call(kernel, "s" + "v" * 7, out, (ids, *terms, *got), 1_000_000, scratch)[0]


def join(pieces):
    def kernel(in_ref, out, total):
        for j in range(8):
            total[j * OWN : (j + 1) * OWN, :] = in_ref[j].astype(F32)
        out[...] = total[...].astype(BF16)

    return call(kernel, "v", [("v", (HALF, 128), BF16)], (pieces,), 300_000, (pltpu.VMEM((HALF, 128), F32),))[0]


def stack(*blocks):
    def kernel(*refs):
        for k in range(2):
            refs[2][k] = refs[k][...]

    return call(kernel, "vv", [("v", (2, HALF, 128), BF16)], blocks, 300_000)[0]


def place(ids, kinds, arrays, out=None):
    jobs = [(k, n) for k, kind in enumerate(kinds) for n in range(len(kind[2]))]

    def kernel(ids_ref, *refs):
        out_ref, sems = refs[-2], refs[-1]
        copies = []
        for s, (k, n) in enumerate(jobs):
            swapped, r, shifts = kinds[k]
            core = ids_ref[0] if swapped == 0 else 1 - ids_ref[0]
            x = lax.rem(ids_ref[4] + jnp.where(core == 0, r, shifts[n]), NX)
            y = lax.rem(ids_ref[5] + jnp.where(core == 0, shifts[n], r), NX)
            src = refs[k] if len(shifts) == 1 else refs[k].at[n]
            copies.append(pltpu.make_async_copy(src, out_ref.at[x, y, core], sems.at[s]))
        for copy in copies:
            copy.start()
        for copy in copies:
            copy.wait()

    more = () if out is None else (out,)
    aliases = {} if out is None else {1 + len(arrays): 0}
    sems = (pltpu.SemaphoreType.DMA((len(jobs),)),)
    outs = [("a", (NX, NX, 2, HALF, 128), BF16)]
    return call(kernel, "s" + "a" * (len(arrays) + len(more)), outs, (ids, *arrays, *more), 5_000_000, sems, aliases)[0]


def adamw(factor, summed, params, moment, second):
    clipped = factor * summed
    moment_out = 0.9 * moment + 0.1 * clipped
    second_out = 0.95 * second + 0.05 * clipped * clipped
    first_fix = 1.0 - 0.9**10
    second_fix = 1.0 - 0.95**10
    update = moment_out / first_fix / (jnp.sqrt(second_out / second_fix) + 1e-08) + 0.1 * params
    return params - 0.001 * update, moment_out, second_out


def body(grads, params, moment, second, teacher):
    x, y, z, c = (lax.axis_index(a) for a in AXES)
    ids = jnp.stack([c, jnp.where(c == 0, x, y), jnp.where(c == 0, y, x), z, x, y]).astype(jnp.int32)

    mine = grads.reshape(NX, NX, 2, HALF, 128)
    order = (*SHIFTS, 0)
    give = pick(ids, mine, order, True)
    theirs = [send(g, SWAP) for g in give]
    keep = pick(ids, mine, order, False)
    got = [send(sum_pair(keep[k], theirs[k], BF16), RINGS[0][r]) for k, r in enumerate(SHIFTS)]
    state = send(jnp.stack([params, moment, second]), TO_HOLDER)
    got[2], state = lax.optimization_barrier((got[2], state))
    terms = (sum_pair(keep[3], theirs[3], F32), *got)
    got = [send(total, RINGS[1][q]) for total, q in zip(sum_ring(ids, terms), SHIFTS)]
    held = jnp.sum(exchange(sum_plane(ids, terms, got), "z"), axis=0)
    summed = send(held, TO_OWNER)

    partial = jnp.sum(held * held, axis=0, keepdims=True)
    everyone = NX * NX * NZ * 2
    squares = jnp.sum(exchange(jnp.broadcast_to(partial, (everyone, 128)), AXES))
    squares, summed = lax.optimization_barrier((squares, summed))
    entries = grads.shape[1] * grads.shape[2]
    factor = 1.0 / jnp.sqrt(squares / jnp.float32(entries) + 1e-06)

    params_out, moment_out, second_out = adamw(factor, summed, params, moment, second)
    teacher_out = 0.9999 * teacher + 0.0001 * params_out

    weights = adamw(factor, held, *state)[0].astype(BF16)
    block = join(exchange(jnp.broadcast_to(weights, (8, OWN, 128)), "z"))
    across = [send(block, RINGS[1][r]) for r in (1, 3, 2)]
    left, left_at = stack(block, across[0]), (0, 3)
    right, right_at = stack(across[1], across[2]), (1, 2)
    up, down = RINGS[0][3], RINGS[0][1]
    near = [send(left, up), send(right, down), send(right, up), send(left, down)]
    far = [send(near[0], up), send(near[1], down)]

    def both(r, at):
        return [(0, r, at), (1, r, at)]

    def pair(v):
        return [v, send(v, SWAP)]

    kinds = [(0, 0, left_at), (0, 0, right_at), (0, 1, left_at), (0, 3, right_at)]
    out = place(ids, kinds, [left, right, near[0], near[1]])
    swapped = [send(after(left, near[2]), SWAP), send(after(right, near[3]), SWAP)] + [send(v, SWAP) for v in near[:2]]
    mine = (params_out, moment_out, second_out, teacher_out)
    far[0], far[1], out, mine = lax.optimization_barrier((far[0], far[1], out, mine))
    kinds = [(1, *kind[1:]) for kind in kinds]
    kinds += [(0, 1, right_at), (0, 3, left_at), (0, 2, left_at), (0, 2, right_at)]
    out = place(ids, kinds, swapped + near[2:] + far, out)
    kinds = [(1, 1, right_at), (1, 3, left_at), (1, 2, left_at), (1, 2, right_at)]
    out = place(ids, kinds, [send(v, SWAP) for v in near[2:] + far], out)
    weights_out = out.reshape(grads.shape[1:])
    return (*mine, weights_out)


def solution(mesh):
    split = Mesh(mesh.devices.reshape(NX, NX, NZ, 2), AXES)
    in_specs = (P(AXES, None, None), P(AXES, None), P(AXES, None), P(AXES, None), P(AXES, None))
    out_specs = (P(AXES, None), P(AXES, None), P(AXES, None), P(AXES, None), P())
    return jax.shard_map(body, mesh=split, in_specs=in_specs, out_specs=out_specs, check_vma=False)
```

```python
import jax
import jax.numpy as jnp
from jax import lax
from jax.experimental import pallas as pl
from jax.experimental.pallas import tpu as pltpu
from jax.sharding import Mesh
from jax.sharding import PartitionSpec as P

AXES = ("x", "y", "z", "c")
NX, NZ = 4, 8
OWN = 81
HALF = 8 * OWN
MIB = 2**20
F32, BF16 = jnp.float32, jnp.bfloat16


def flat(x, y, z, c):
    return ((x * NX + y) * NZ + z) * 2 + c


def perm_of(step):
    everyone = [(x, y, z, c) for x in range(NX) for y in range(NX) for z in range(NZ) for c in range(2)]
    return [(flat(*d), flat(*step(*d))) for d in everyone]


def ring(level, r):
    def step(x, y, z, c):
        if c == level:
            return (x + r) % NX, y, z, c
        return x, (y + r) % NX, z, c

    return perm_of(step)


def owner(x, y, z, c):
    return x, y, 4 * c + z // 2, z % 2


SWAP = perm_of(lambda x, y, z, c: (x, y, z, 1 - c))
RINGS = [[ring(level, r) for r in range(NX)] for level in range(2)]
TO_OWNER = perm_of(owner)
TO_HOLDER = [(b, a) for a, b in TO_OWNER]
SHIFTS = (2, 1, 3)


def send(x, perm):
    return lax.ppermute(x, AXES, perm)


def after(x, *others):
    return lax.optimization_barrier((x, *others))[0]


def exchange(x, axes):
    return lax.all_to_all(x, axes, split_axis=0, concat_axis=0, tiled=True)


def call(kernel, ins, outs, arrays, cost, scratch=(), aliases=None, vmem=24):
    spaces = {"s": pltpu.SMEM, "v": pltpu.VMEM, "a": pl.ANY, "h": pltpu.HBM}
    return pl.pallas_call(
        kernel,
        in_specs=[pl.BlockSpec(memory_space=spaces[k]) for k in ins],
        out_specs=[pl.BlockSpec(memory_space=spaces[k]) for k, _, _ in outs],
        out_shape=[jax.ShapeDtypeStruct(shape, dtype) for _, shape, dtype in outs],
        scratch_shapes=list(scratch),
        input_output_aliases=aliases or {},
        compiler_params=pltpu.CompilerParams(vmem_limit_bytes=vmem * MIB),
        cost_estimate=pl.CostEstimate(flops=cost, bytes_accessed=cost, transcendentals=0),
    )(*arrays)


def pick(ids, mine, shifts, give):
    def kernel(ids_ref, mine_ref, *refs):
        outs, sems = refs[:-1], refs[-1]
        core = 1 - ids_ref[0] if give else ids_ref[0]
        on_x = core == 0
        copies = []
        for k, r in enumerate(shifts):
            first = lax.rem(jnp.where(on_x, ids_ref[4], ids_ref[5]) + r, NX)
            for j in range(NX):
                at = jnp.where(on_x, first, j), jnp.where(on_x, j, first)
                copies.append(pltpu.make_async_copy(mine_ref.at[at[0], at[1], core], outs[k].at[j], sems.at[4 * k + j]))
        for copy in copies:
            copy.start()
        for copy in copies:
            copy.wait()

    outs = [("v", (NX, HALF, 128), BF16)] * len(shifts)
    sems = (pltpu.SemaphoreType.DMA((4 * len(shifts),)),)
    return call(kernel, "sh", outs, (ids, mine), 1_000_000 * len(shifts), sems, vmem=50 if give else 48)


def sum_pair(keep, theirs, dtype):
    def kernel(a_ref, b_ref, o_ref):
        @pl.loop(0, NX)
        def _(j):
            o_ref[j] = (a_ref[j].astype(F32) + b_ref[j].astype(F32)).astype(dtype)

    return call(kernel, "vv", [("v", (NX, HALF, 128), dtype)], (keep, theirs), 1_000_000)[0]


def ring_total(j, refs):
    total = refs[0][j]
    for ref in refs[1:]:
        total = total + ref[j].astype(F32)
    return total


def sum_ring(ids, terms):
    def kernel(ids_ref, *refs):
        for q, out in zip(SHIFTS, refs[4:]):
            out[...] = ring_total(lax.rem(ids_ref[2] + q, NX), refs[:4])

    return call(kernel, "s" + "v" * 4, [("v", (HALF, 128), F32)] * 3, (ids, *terms), 1_000_000)


def sum_plane(ids, terms, got):
    def kernel(ids_ref, *refs):
        out, total = refs[-2:]
        total[...] = ring_total(ids_ref[2], refs[:4]) + refs[4][...] + refs[5][...] + refs[6][...]
        for j in range(8):
            out[j] = total[j * OWN : (j + 1) * OWN, :]

    out = [("v", (8, OWN, 128), F32)]
    scratch = (pltpu.VMEM((HALF, 128), F32),)
    return call(kernel, "s" + "v" * 7, out, (ids, *terms, *got), 1_000_000, scratch)[0]


def join(pieces):
    def kernel(in_ref, out, total):
        for j in range(8):
            total[j * OWN : (j + 1) * OWN, :] = in_ref[j].astype(F32)
        out[...] = total[...].astype(BF16)

    return call(kernel, "v", [("v", (HALF, 128), BF16)], (pieces,), 300_000, (pltpu.VMEM((HALF, 128), F32),))[0]


def stack(*blocks):
    def kernel(*refs):
        for k in range(2):
            refs[2][k] = refs[k][...]

    return call(kernel, "vv", [("v", (2, HALF, 128), BF16)], blocks, 300_000)[0]


def place(ids, kinds, arrays, out=None):
    jobs = [(k, n) for k, kind in enumerate(kinds) for n in range(len(kind[2]))]

    def kernel(ids_ref, *refs):
        out_ref, sems = refs[-2], refs[-1]
        copies = []
        for s, (k, n) in enumerate(jobs):
            swapped, r, shifts = kinds[k]
            core = ids_ref[0] if swapped == 0 else 1 - ids_ref[0]
            x = lax.rem(ids_ref[4] + jnp.where(core == 0, r, shifts[n]), NX)
            y = lax.rem(ids_ref[5] + jnp.where(core == 0, shifts[n], r), NX)
            src = refs[k] if len(shifts) == 1 else refs[k].at[n]
            copies.append(pltpu.make_async_copy(src, out_ref.at[x, y, core], sems.at[s]))
        for copy in copies:
            copy.start()
        for copy in copies:
            copy.wait()

    more = () if out is None else (out,)
    aliases = {} if out is None else {1 + len(arrays): 0}
    sems = (pltpu.SemaphoreType.DMA((len(jobs),)),)
    outs = [("a", (NX, NX, 2, HALF, 128), BF16)]
    return call(kernel, "s" + "a" * (len(arrays) + len(more)), outs, (ids, *arrays, *more), 5_000_000, sems, aliases)[0]


def adamw(factor, summed, params, moment, second):
    clipped = factor * summed
    moment_out = 0.9 * moment + 0.1 * clipped
    second_out = 0.95 * second + 0.05 * clipped * clipped
    first_fix = 1.0 - 0.9**10
    second_fix = 1.0 - 0.95**10
    update = moment_out / first_fix / (jnp.sqrt(second_out / second_fix) + 1e-08) + 0.1 * params
    return params - 0.001 * update, moment_out, second_out


def body(grads, params, moment, second, teacher):
    x, y, z, c = (lax.axis_index(a) for a in AXES)
    ids = jnp.stack([c, jnp.where(c == 0, x, y), jnp.where(c == 0, y, x), z, x, y]).astype(jnp.int32)

    mine = grads.reshape(NX, NX, 2, HALF, 128)
    order = (*SHIFTS, 0)
    give = pick(ids, mine, order, True)
    theirs = [send(g, SWAP) for g in give]
    keep = pick(ids, mine, order, False)
    got = [send(sum_pair(keep[k], theirs[k], BF16), RINGS[0][r]) for k, r in enumerate(SHIFTS)]
    state = send(jnp.stack([params, moment, second]), TO_HOLDER)
    got[2], state = lax.optimization_barrier((got[2], state))
    terms = (sum_pair(keep[3], theirs[3], F32), *got)
    got = [send(total, RINGS[1][q]) for total, q in zip(sum_ring(ids, terms), SHIFTS)]
    held = jnp.sum(exchange(sum_plane(ids, terms, got), "z"), axis=0)
    summed = send(held, TO_OWNER)

    partial = jnp.sum(held * held, axis=0, keepdims=True)
    everyone = NX * NX * NZ * 2
    squares = jnp.sum(exchange(jnp.broadcast_to(partial, (everyone, 128)), AXES))
    squares, summed = lax.optimization_barrier((squares, summed))
    entries = grads.shape[1] * grads.shape[2]
    factor = 1.0 / jnp.sqrt(squares / jnp.float32(entries) + 1e-06)

    params_out, moment_out, second_out = adamw(factor, summed, params, moment, second)
    teacher_out = 0.9999 * teacher + 0.0001 * params_out

    weights = adamw(factor, held, *state)[0].astype(BF16)
    block = join(exchange(jnp.broadcast_to(weights, (8, OWN, 128)), "z"))
    across = [send(block, RINGS[1][r]) for r in (2, 1, 3)]
    left, left_at = stack(block, across[0]), (0, 2)
    right, right_at = stack(across[1], across[2]), (3, 1)
    up, down = RINGS[0][3], RINGS[0][1]
    near = [send(left, up), send(right, down), send(right, up), send(left, down)]
    far = [send(near[0], up), send(near[1], down)]

    def both(r, at):
        return [(0, r, at), (1, r, at)]

    def pair(v):
        return [v, send(v, SWAP)]

    kinds = [(0, 0, left_at), (0, 0, right_at), (0, 1, left_at), (0, 3, right_at)]
    out = place(ids, kinds, [left, right, near[0], near[1]])
    swapped = [send(after(left, near[2]), SWAP), send(after(right, near[3]), SWAP)] + [send(v, SWAP) for v in near[:2]]
    mine = (params_out, moment_out, second_out, teacher_out)
    far[0], far[1], out, mine = lax.optimization_barrier((far[0], far[1], out, mine))
    kinds = [(1, *kind[1:]) for kind in kinds]
    kinds += [(0, 1, right_at), (0, 3, left_at), (0, 2, left_at), (0, 2, right_at)]
    out = place(ids, kinds, swapped + near[2:] + far, out)
    kinds = [(1, 1, right_at), (1, 3, left_at), (1, 2, left_at), (1, 2, right_at)]
    out = place(ids, kinds, [send(v, SWAP) for v in near[2:] + far], out)
    weights_out = out.reshape(grads.shape[1:])
    return (*mine, weights_out)


def solution(mesh):
    split = Mesh(mesh.devices.reshape(NX, NX, NZ, 2), AXES)
    in_specs = (P(AXES, None, None), P(AXES, None), P(AXES, None), P(AXES, None), P(AXES, None))
    out_specs = (P(AXES, None), P(AXES, None), P(AXES, None), P(AXES, None), P())
    return jax.shard_map(body, mesh=split, in_specs=in_specs, out_specs=out_specs, check_vma=False)
```

```python
import jax
import jax.numpy as jnp
from jax import lax
from jax.experimental import pallas as pl
from jax.experimental.pallas import tpu as pltpu
from jax.sharding import Mesh
from jax.sharding import PartitionSpec as P

AXES = ("x", "y", "z", "c")
NX, NZ = 4, 8
OWN = 81
HALF = 8 * OWN
MIB = 2**20
F32, BF16 = jnp.float32, jnp.bfloat16


def flat(x, y, z, c):
    return ((x * NX + y) * NZ + z) * 2 + c


def perm_of(step):
    everyone = [(x, y, z, c) for x in range(NX) for y in range(NX) for z in range(NZ) for c in range(2)]
    return [(flat(*d), flat(*step(*d))) for d in everyone]


def ring(level, r):
    def step(x, y, z, c):
        if c == level:
            return (x + r) % NX, y, z, c
        return x, (y + r) % NX, z, c

    return perm_of(step)


def owner(x, y, z, c):
    return x, y, 4 * c + z // 2, z % 2


SWAP = perm_of(lambda x, y, z, c: (x, y, z, 1 - c))
RINGS = [[ring(level, r) for r in range(NX)] for level in range(2)]
TO_OWNER = perm_of(owner)
TO_HOLDER = [(b, a) for a, b in TO_OWNER]
SHIFTS = (1, 3, 2)


def send(x, perm):
    return lax.ppermute(x, AXES, perm)


def after(x, *others):
    return lax.optimization_barrier((x, *others))[0]


def exchange(x, axes):
    return lax.all_to_all(x, axes, split_axis=0, concat_axis=0, tiled=True)


def call(kernel, ins, outs, arrays, cost, scratch=(), aliases=None, vmem=24):
    spaces = {"s": pltpu.SMEM, "v": pltpu.VMEM, "a": pl.ANY, "h": pltpu.HBM}
    return pl.pallas_call(
        kernel,
        in_specs=[pl.BlockSpec(memory_space=spaces[k]) for k in ins],
        out_specs=[pl.BlockSpec(memory_space=spaces[k]) for k, _, _ in outs],
        out_shape=[jax.ShapeDtypeStruct(shape, dtype) for _, shape, dtype in outs],
        scratch_shapes=list(scratch),
        input_output_aliases=aliases or {},
        compiler_params=pltpu.CompilerParams(vmem_limit_bytes=vmem * MIB),
        cost_estimate=pl.CostEstimate(flops=cost, bytes_accessed=cost, transcendentals=0),
    )(*arrays)


def pick(ids, mine, shifts, give):
    def kernel(ids_ref, mine_ref, *refs):
        outs, sems = refs[:-1], refs[-1]
        core = 1 - ids_ref[0] if give else ids_ref[0]
        on_x = core == 0
        copies = []
        for k, r in enumerate(shifts):
            first = lax.rem(jnp.where(on_x, ids_ref[4], ids_ref[5]) + r, NX)
            for j in range(NX):
                at = jnp.where(on_x, first, j), jnp.where(on_x, j, first)
                copies.append(pltpu.make_async_copy(mine_ref.at[at[0], at[1], core], outs[k].at[j], sems.at[4 * k + j]))
        for copy in copies:
            copy.start()
        for copy in copies:
            copy.wait()

    outs = [("v", (NX, HALF, 128), BF16)] * len(shifts)
    sems = (pltpu.SemaphoreType.DMA((4 * len(shifts),)),)
    return call(kernel, "sh", outs, (ids, mine), 1_000_000 * len(shifts), sems, vmem=50 if give else 48)


def sum_pair(keep, theirs, dtype):
    def kernel(a_ref, b_ref, o_ref):
        @pl.loop(0, NX)
        def _(j):
            o_ref[j] = (a_ref[j].astype(F32) + b_ref[j].astype(F32)).astype(dtype)

    return call(kernel, "vv", [("v", (NX, HALF, 128), dtype)], (keep, theirs), 1_000_000)[0]


def ring_total(j, refs):
    total = refs[0][j]
    for ref in refs[1:]:
        total = total + ref[j].astype(F32)
    return total


def sum_ring(ids, terms):
    def kernel(ids_ref, *refs):
        for q, out in zip(SHIFTS, refs[4:]):
            out[...] = ring_total(lax.rem(ids_ref[2] + q, NX), refs[:4])

    return call(kernel, "s" + "v" * 4, [("v", (HALF, 128), F32)] * 3, (ids, *terms), 1_000_000)


def sum_plane(ids, terms, got):
    def kernel(ids_ref, *refs):
        out, total = refs[-2:]
        total[...] = ring_total(ids_ref[2], refs[:4]) + refs[4][...] + refs[5][...] + refs[6][...]
        for j in range(8):
            out[j] = total[j * OWN : (j + 1) * OWN, :]

    out = [("v", (8, OWN, 128), F32)]
    scratch = (pltpu.VMEM((HALF, 128), F32),)
    return call(kernel, "s" + "v" * 7, out, (ids, *terms, *got), 1_000_000, scratch)[0]


def join(pieces):
    def kernel(in_ref, out, total):
        for j in range(8):
            total[j * OWN : (j + 1) * OWN, :] = in_ref[j].astype(F32)
        out[...] = total[...].astype(BF16)

    return call(kernel, "v", [("v", (HALF, 128), BF16)], (pieces,), 300_000, (pltpu.VMEM((HALF, 128), F32),))[0]


def stack(*blocks):
    def kernel(*refs):
        for k in range(2):
            refs[2][k] = refs[k][...]

    return call(kernel, "vv", [("v", (2, HALF, 128), BF16)], blocks, 300_000)[0]


def place(ids, kinds, arrays, out=None):
    jobs = [(k, n) for k, kind in enumerate(kinds) for n in range(len(kind[2]))]

    def kernel(ids_ref, *refs):
        out_ref, sems = refs[-2], refs[-1]
        copies = []
        for s, (k, n) in enumerate(jobs):
            swapped, r, shifts = kinds[k]
            core = ids_ref[0] if swapped == 0 else 1 - ids_ref[0]
            x = lax.rem(ids_ref[4] + jnp.where(core == 0, r, shifts[n]), NX)
            y = lax.rem(ids_ref[5] + jnp.where(core == 0, shifts[n], r), NX)
            src = refs[k] if len(shifts) == 1 else refs[k].at[n]
            copies.append(pltpu.make_async_copy(src, out_ref.at[x, y, core], sems.at[s]))
        for copy in copies:
            copy.start()
        for copy in copies:
            copy.wait()

    more = () if out is None else (out,)
    aliases = {} if out is None else {1 + len(arrays): 0}
    sems = (pltpu.SemaphoreType.DMA((len(jobs),)),)
    outs = [("a", (NX, NX, 2, HALF, 128), BF16)]
    return call(kernel, "s" + "a" * (len(arrays) + len(more)), outs, (ids, *arrays, *more), 5_000_000, sems, aliases)[0]


def adamw(factor, summed, params, moment, second):
    clipped = factor * summed
    moment_out = 0.9 * moment + 0.1 * clipped
    second_out = 0.95 * second + 0.05 * clipped * clipped
    first_fix = 1.0 - 0.9**10
    second_fix = 1.0 - 0.95**10
    update = moment_out / first_fix / (jnp.sqrt(second_out / second_fix) + 1e-08) + 0.1 * params
    return params - 0.001 * update, moment_out, second_out


def body(grads, params, moment, second, teacher):
    x, y, z, c = (lax.axis_index(a) for a in AXES)
    ids = jnp.stack([c, jnp.where(c == 0, x, y), jnp.where(c == 0, y, x), z, x, y]).astype(jnp.int32)

    mine = grads.reshape(NX, NX, 2, HALF, 128)
    order = (*SHIFTS, 0)
    give = pick(ids, mine, order, True)
    theirs = [send(g, SWAP) for g in give]
    keep = pick(ids, mine, order, False)
    got = [send(sum_pair(keep[k], theirs[k], BF16), RINGS[0][r]) for k, r in enumerate(SHIFTS)]
    state = send(jnp.stack([params, moment, second]), TO_HOLDER)
    got[2], state = lax.optimization_barrier((got[2], state))
    terms = (sum_pair(keep[3], theirs[3], F32), *got)
    got = [send(total, RINGS[1][q]) for total, q in zip(sum_ring(ids, terms), SHIFTS)]
    held = jnp.sum(exchange(sum_plane(ids, terms, got), "z"), axis=0)
    summed = send(held, TO_OWNER)

    partial = jnp.sum(held * held, axis=0, keepdims=True)
    everyone = NX * NX * NZ * 2
    squares = jnp.sum(exchange(jnp.broadcast_to(partial, (everyone, 128)), AXES))
    squares, summed = lax.optimization_barrier((squares, summed))
    entries = grads.shape[1] * grads.shape[2]
    factor = 1.0 / jnp.sqrt(squares / jnp.float32(entries) + 1e-06)

    params_out, moment_out, second_out = adamw(factor, summed, params, moment, second)
    teacher_out = 0.9999 * teacher + 0.0001 * params_out

    weights = adamw(factor, held, *state)[0].astype(BF16)
    block = join(exchange(jnp.broadcast_to(weights, (8, OWN, 128)), "z"))
    across = [send(block, RINGS[1][r]) for r in (2, 1, 3)]
    left, left_at = stack(block, across[0]), (0, 2)
    right, right_at = stack(across[1], across[2]), (3, 1)
    up, down = RINGS[0][3], RINGS[0][1]
    near = [send(left, up), send(right, down), send(right, up), send(left, down)]
    far = [send(near[0], up), send(near[1], down)]

    def both(r, at):
        return [(0, r, at), (1, r, at)]

    def pair(v):
        return [v, send(v, SWAP)]

    kinds = [(0, 0, left_at), (0, 0, right_at), (0, 1, left_at), (0, 3, right_at)]
    out = place(ids, kinds, [left, right, near[0], near[1]])
    swapped = [send(after(left, near[2]), SWAP), send(after(right, near[3]), SWAP)] + [send(v, SWAP) for v in near[:2]]
    mine = (params_out, moment_out, second_out, teacher_out)
    far[0], far[1], out, mine = lax.optimization_barrier((far[0], far[1], out, mine))
    kinds = [(1, *kind[1:]) for kind in kinds]
    kinds += [(0, 1, right_at), (0, 3, left_at), (0, 2, left_at), (0, 2, right_at)]
    out = place(ids, kinds, swapped + near[2:] + far, out)
    kinds = [(1, 1, right_at), (1, 3, left_at), (1, 2, left_at), (1, 2, right_at)]
    out = place(ids, kinds, [send(v, SWAP) for v in near[2:] + far], out)
    weights_out = out.reshape(grads.shape[1:])
    return (*mine, weights_out)


def solution(mesh):
    split = Mesh(mesh.devices.reshape(NX, NX, NZ, 2), AXES)
    in_specs = (P(AXES, None, None), P(AXES, None), P(AXES, None), P(AXES, None), P(AXES, None))
    out_specs = (P(AXES, None), P(AXES, None), P(AXES, None), P(AXES, None), P())
    return jax.shard_map(body, mesh=split, in_specs=in_specs, out_specs=out_specs, check_vma=False)
```
